256 devices in a mesh: dp: 16 (over y, x), fsdp: 16 (over z, core).
Axes of the slice: x: 4, y: 4, z: 8, core: 2. Of those that a mesh axis runs over, the one named last changes fastest.
Arguments:
- grads: bfloat16 [16, 16, 1408, 2048], P('dp', None, 'fsdp')
- momentum: float32 [16, 1408, 2048], P(None, 'fsdp', 'dp')
- weights: bfloat16 [16, 1408, 2048], P(None, 'fsdp', 'dp'), may hold values from -0.125 to 0.125
Outputs:
- moment_new: float32 [16, 1408, 2048], P(None, 'fsdp', 'dp')
- new_weights: bfloat16 [16, 1408, 2048], P(None, 'fsdp', 'dp')
- update: bfloat16 [16, 1408, 2048], P(None, 'fsdp', 'dp')
The draws below stay inside these ranges and needn't reach their ends.
All inputs are finite; a program needn't handle non-finite values.
Results may differ from the reference program's by a relative error of at most 0.03.
Values may be sent and summed in bfloat16 or wider, within the bound.
No kernel may reach another device: no remote copies, remote signals or barrier semaphores. Data moves between devices by JAX's collectives and lax.ppermute only.
A program may use at most 64 MiB of HBM per device.

```python
import math
import jax
import jax.numpy as jnp
from jax import lax

ROWS = 1408
COLS = 2048
NS_ITERS = 2
NMAT = 16
N_DP = 16


SHARE_RATIO = 0.43


def factors(key, count, top):
    return jnp.exp(jax.random.uniform(key, (count,), jnp.float32) * jnp.log(top)) / jnp.sqrt(top)


def mean_square(top):
    return (top * top - 1.0) / (2.0 * math.log(top) * top)


def draw_grads(key, part):
    key = jax.random.fold_in(key, 11)
    keys = jax.random.split(key, 3)
    rising = 3.0 ** (jnp.arange(COLS, dtype=jnp.float32) / COLS) / jnp.sqrt(3.0)
    col_scale = factors(keys[1], COLS, 10.0) * rising
    row_scale = factors(keys[0], ROWS, 10.0)
    noise = jax.random.normal(keys[2], (N_DP, NMAT, ROWS, COLS), jnp.float32)
    return (noise * row_scale[:, None] * col_scale[None, :]).astype(jnp.bfloat16)


def draw_momentum(key, part):
    key = jax.random.fold_in(key, 23)
    keys = jax.random.split(key, 5)
    rising = 3.0 ** (jnp.arange(COLS, dtype=jnp.float32) / COLS) / jnp.sqrt(3.0)
    col_scale = factors(keys[1], COLS, 10.0) * rising
    left = jax.random.normal(keys[3], (NMAT, ROWS), jnp.float32)
    right = jax.random.normal(keys[4], (NMAT, COLS), jnp.float32) * col_scale[None, :]
    row_scale = factors(keys[0], ROWS, 10.0)
    noise = 2.0 * jax.random.normal(keys[2], (NMAT, ROWS, COLS), jnp.float32)
    spread = N_DP + 0.9025 * 4.0
    energy = mean_square(10.0) * spread
    amplitude = math.sqrt(SHARE_RATIO * energy / 0.9025)
    shared = amplitude * left[:, :, None] * right[:, None, :]
    return noise * row_scale[:, None] * col_scale[None, :] + shared


def level_of(stream_key, extent, shards, least, largest):
    gain, own = 1.0, jax.random.fold_in(stream_key, 6)
    for dim, shards_of in shards:
        draws = jnp.exp(jax.random.uniform(jax.random.fold_in(own, dim), (shards_of,), jnp.float32, least / len(shards), largest / len(shards)))
        gain = gain * jnp.repeat(draws, extent[dim] // shards_of).reshape([-1 if axis == dim else 1 for axis in range(len(extent))])
    return gain


def bell_draw(key, dims, scale, most, cuts=(), kind=jnp.bfloat16):
    array = scale * jax.random.normal(key, dims, jnp.float32)
    if cuts:
        array = array * level_of(key, dims, cuts, -0.22, 0.18)
    return jnp.clip(array, -most, most).astype(kind)


def setup_inputs(seed: int = 0) -> dict:
    streams_of = jax.random.split(jax.random.key(seed), 4)
    grads = draw_grads(jax.random.fold_in(streams_of[3], 71), 0)
    momentum = draw_momentum(jax.random.fold_in(streams_of[3], 71), 0)
    weights = bell_draw(streams_of[2], (NMAT, ROWS, COLS), COLS ** -0.5, 0.125, ((1, 16), (2, 16)))
    return {"grads": grads, "momentum": momentum, "weights": weights}


MOMENTUM_DECAY = 0.95
LEARN_RATE = 0.02
DECAY_RATE = 0.1
COEF_A = 3.4445
COEF_B = -4.775
COEF_C = 2.0315
EPS_NORM = 1e-07

def orthogonalize(sent):
    wide = sent.astype(jnp.float32)
    total = jnp.sum(wide * wide)
    current = (wide / (jnp.sqrt(total) + EPS_NORM)).astype(jnp.bfloat16)
    width = COLS // N_DP
    for step in range(NS_ITERS):
        gram = jnp.zeros((ROWS, ROWS), jnp.float32)
        for block in range(N_DP):
            columns = current[:, block * width:(block + 1) * width]
            term = jnp.dot(columns, columns.T, preferred_element_type=jnp.float32)
            term = lax.optimization_barrier(term.astype(jnp.bfloat16))
            gram = gram + term.astype(jnp.float32)
        gram = gram.astype(jnp.bfloat16)
        once = jnp.dot(gram, current, preferred_element_type=jnp.float32).astype(jnp.bfloat16)
        twice = jnp.dot(gram, once, preferred_element_type=jnp.float32)
        current = (COEF_A * current.astype(jnp.float32) + COEF_B * once.astype(jnp.float32) + COEF_C * twice).astype(jnp.bfloat16)
    return current

def reference(grads, momentum, weights):
    scale = 0.2 * math.sqrt(max(ROWS, COLS))

    def single(index):
        gradient = lax.optimization_barrier(jnp.sum(lax.dynamic_index_in_dim(grads, index, 1, keepdims=False).astype(jnp.float32), axis=0))
        moment_new = MOMENTUM_DECAY * lax.dynamic_index_in_dim(momentum, index, 0, keepdims=False) + gradient
        result = orthogonalize(moment_new.astype(jnp.bfloat16))
        direction = scale * result.astype(jnp.float32)
        previous = lax.dynamic_index_in_dim(weights, index, 0, keepdims=False).astype(jnp.float32)
        new_weights = (previous * (1.0 - LEARN_RATE * DECAY_RATE) - LEARN_RATE * direction).astype(jnp.bfloat16)
        return (moment_new, new_weights, direction.astype(jnp.bfloat16))
    moments, updated, steps_out = lax.map(single, jnp.arange(NMAT, dtype=jnp.int32))
    return (moments, updated, steps_out)
```

```python
import functools
import math

import jax
import jax.numpy as jnp
from jax import lax
from jax.experimental import pallas as pl
from jax.experimental.pallas import tpu as pltpu
from jax.sharding import PartitionSpec as P

NS_ITERS = 2
SIDE = 4

MOMENTUM_DECAY = 0.95
LEARN_RATE = 0.02
DECAY_RATE = 0.1
COEF_A = 3.4445
COEF_B = -4.775
COEF_C = 2.0315
EPS_NORM = 1e-07
F32 = jnp.float32
BF16 = jnp.bfloat16


def shift(value, dx, dy):
    pairs = []
    for y in range(SIDE):
        for x in range(SIDE):
            there = ((y + dy) % SIDE) * SIDE + (x + dx) % SIDE
            pairs.append((y * SIDE + x, there))
    return lax.ppermute(value, "dp", pairs)


def add_up(parts):
    total = parts[0].astype(F32)
    for part in parts[1:]:
        total = total + part.astype(F32)
    return total


def combine_kernel(*refs):
    half_a, half_b, mom, blocks, rows = refs[:4], refs[4:8], refs[8], refs[9], refs[10]
    count = blocks.shape[0]
    wide = half_a[0].shape[-1]
    per = wide // 128
    for block in range(count):
        terms = half_a if block < per else half_b
        col = (block % per) * 128
        total = add_up([ref[:, col : col + 128] for ref in terms])
        blocks[block] = total.astype(BF16)
        moment = MOMENTUM_DECAY * mom[block] + total.astype(BF16).astype(F32)
        rows[:, block * 128 : (block + 1) * 128] = moment.astype(BF16)


def combine(half_a, half_b, mom):
    count, rows, _ = mom.shape
    return pl.pallas_call(
        combine_kernel,
        out_shape=(
            jax.ShapeDtypeStruct((count, rows, 128), BF16),
            jax.ShapeDtypeStruct((rows, count * 128), BF16),
        ),
        in_specs=[pl.BlockSpec(memory_space=pltpu.VMEM)] * 9,
        out_specs=(pl.BlockSpec(memory_space=pltpu.VMEM),) * 2,
        compiler_params=pltpu.CompilerParams(vmem_limit_bytes=16 << 20),
    )(*half_a, *half_b, mom)


def newton_schulz_kernel(mine, sent, out, gram, state):
    size = sent.shape[0]
    rows = out.shape[1]
    tiles = [(at, min(256, size - at)) for at in range(0, size, 256)]
    total = jnp.zeros((1, 1), F32)
    raw = []
    for at, high in tiles:
        term = lax.dot_general(
            sent[pl.ds(at, high), :], sent[...], (((1,), (1,)), ((), ())), preferred_element_type=F32
        )
        here = lax.broadcasted_iota(jnp.int32, (high, size), 0) + at
        there = lax.broadcasted_iota(jnp.int32, (high, size), 1)
        total = total + jnp.sum(jnp.where(here == there, term, 0.0), keepdims=True)
        state[pl.ds(at, high), :] = term
    finite = total < jnp.inf
    inverse = 1.0 / (jnp.sqrt(total) + EPS_NORM)
    for at, high in tiles:
        scaled = state[pl.ds(at, high), :] * inverse * inverse
        gram[pl.ds(at, high), :] = jnp.where(finite, scaled, 0.0).astype(BF16)

    def times_gram(value):
        high = value.astype(BF16)
        low = (value - high.astype(F32)).astype(BF16)
        both = jnp.dot(gram[...], jnp.concatenate([high, low], axis=1), preferred_element_type=F32)
        return both[:, :128] + both[:, 128:]

    def poly(times, value):
        once = times(value)
        twice = times(once)
        return COEF_A * value + COEF_B * once + COEF_C * twice

    first = mine[0] * rows
    unit = (
        lax.broadcasted_iota(jnp.int32, (size, 128), 0) - first
        == lax.broadcasted_iota(jnp.int32, (size, 128), 1)
    ).astype(F32)
    value = poly(times_gram, unit)
    value = poly(lambda v: poly(times_gram, times_gram(poly(times_gram, v))), value)
    weights = value.T[:rows]
    high = weights.astype(BF16)
    low = (weights - high.astype(F32)).astype(BF16)
    result = jnp.dot(high, sent[...], preferred_element_type=F32)
    result = result + jnp.dot(low, sent[...], preferred_element_type=F32)
    result = (result * inverse).astype(BF16)
    for block in range(out.shape[0]):
        out[block] = result[:, block * 128 : (block + 1) * 128]


def newton_schulz(mine, sent, rows):
    size, wide = sent.shape
    return pl.pallas_call(
        newton_schulz_kernel,
        out_shape=jax.ShapeDtypeStruct((wide // 128, rows, 128), BF16),
        in_specs=[pl.BlockSpec(memory_space=pltpu.SMEM), pl.BlockSpec(memory_space=pltpu.VMEM)],
        out_specs=pl.BlockSpec(memory_space=pltpu.VMEM),
        scratch_shapes=[pltpu.VMEM((size, size), BF16), pltpu.VMEM((size, size), F32)],
        compiler_params=pltpu.CompilerParams(vmem_limit_bytes=48 << 20),
    )(mine, sent)


def body(grads, momentum, weights):
    mat_count, rows_dev, cols_dev = momentum.shape
    owner_count = lax.axis_size("fsdp")
    rows_total = rows_dev * owner_count
    cols_total = cols_dev * lax.axis_size("dp")
    half = cols_total // 2
    place = lax.axis_index("dp")
    y, x = place // SIDE, place % SIDE
    grid = grads[0].reshape(SIDE, SIDE, rows_dev, cols_total)

    mom = lax.all_to_all(momentum, "dp", split_axis=0, concat_axis=0, tiled=True)

    def to_x(k):
        return lax.dynamic_index_in_dim(grid[..., :half], (x + k) % SIDE, 1, keepdims=False)

    def to_y(k):
        return lax.dynamic_index_in_dim(grid[..., half:], (y + k) % SIDE, 0, keepdims=False)

    got_a = [shift(to_x(k), k, 0) for k in (2, 1, 3)]
    got_b = [shift(to_y(k), 0, k) for k in (2, 1, 3)]
    part_a = add_up([to_x(0)] + got_a).astype(BF16)
    part_b = add_up([to_y(0)] + got_b).astype(BF16)

    def of_a(k):
        return lax.dynamic_index_in_dim(part_a, (y + k) % SIDE, 0, keepdims=False)

    def of_b(k):
        return lax.dynamic_index_in_dim(part_b, (x + k) % SIDE, 0, keepdims=False)

    half_a = [of_a(0)] + [shift(of_a(k), 0, k) for k in (2, 1, 3)]
    half_b = [of_b(0)] + [shift(of_b(k), k, 0) for k in (2, 1, 3)]
    blocks, sent = combine(half_a, half_b, mom)

    gathered = lax.all_gather(sent, "fsdp", axis=0, tiled=True)
    summed = lax.all_to_all(blocks, "dp", split_axis=0, concat_axis=0, tiled=True)
    moment_new = MOMENTUM_DECAY * momentum + summed.astype(F32)

    mine = lax.axis_index("fsdp").astype(jnp.int32).reshape(1)
    current = newton_schulz(mine, gathered, rows_dev)
    returned = lax.all_to_all(current, "dp", split_axis=0, concat_axis=0, tiled=True)
    scale = 0.2 * math.sqrt(max(rows_total, cols_total))
    direction = scale * returned.astype(F32)
    new_weights = (
        weights.astype(F32) * (1.0 - LEARN_RATE * DECAY_RATE) - LEARN_RATE * direction
    ).astype(BF16)
    return (moment_new, new_weights, direction.astype(BF16))


def solution(mesh):
    placed = (P("dp", None, "fsdp", None), P(None, "fsdp", "dp"), P(None, "fsdp", "dp"))
    return jax.shard_map(
        body,
        mesh=mesh,
        in_specs=placed,
        out_specs=(P(None, "fsdp", "dp"), P(None, "fsdp", "dp"), P(None, "fsdp", "dp")),
        check_vma=False,
    )
```

```python
import functools
import math

import jax
import jax.numpy as jnp
from jax import lax
from jax.experimental import pallas as pl
from jax.experimental.pallas import tpu as pltpu
from jax.sharding import PartitionSpec as P

NS_ITERS = 2
SIDE = 4
RING = 8
PIECES = RING + 1
LANE = 128
HALVES = 2

MOMENTUM_DECAY = 0.95
LEARN_RATE = 0.02
DECAY_RATE = 0.1
COEF_A = 3.4445
COEF_B = -4.775
COEF_C = 2.0315
EPS_NORM = 1e-07
F32 = jnp.float32
BF16 = jnp.bfloat16
ROWS_BY_ROWS = (((1,), (1,)), ((), ()))
ANYWHERE = pl.BlockSpec(memory_space=pl.ANY)
IN_HBM = pl.BlockSpec(memory_space=pltpu.HBM)
IN_VMEM = pl.BlockSpec(memory_space=pltpu.VMEM)


def move(value, target):
    pairs = []
    for y in range(SIDE):
        for x in range(SIDE):
            for z in range(RING):
                for core in range(2):
                    ty, tx, tz, tc = target(y, x, z, core)
                    there = (((ty % SIDE) * SIDE + tx % SIDE) * RING + tz % RING) * 2 + tc % 2
                    pairs.append((((y * SIDE + x) * RING + z) * 2 + core, there))
    return lax.ppermute(value, ("dp", "fsdp"), pairs)


def first_hop(value, k):
    return move(value, lambda y, x, z, c: (y, x + k, z, c) if c == 0 else (y + k, x, z, c))


def second_hop(value, k):
    return move(value, lambda y, x, z, c: (y + k, x, z, c) if c == 0 else (y, x + k, z, c))


def along_z(value, k):
    return move(value, lambda y, x, z, c: (y, x, z + k, c) if c == 0 else (y, x, z - k, c))


def swap(value):
    return move(value, lambda y, x, z, c: (y, x, z, c + 1))


def cost(flops, size):
    return pl.CostEstimate(flops=flops, bytes_accessed=size, transcendentals=0)


def matrix(k, m):
    place = lax.axis_index("dp")
    y, x = place // SIDE, place % SIDE
    by_x = ((y + m) % SIDE) * SIDE + (x + k) % SIDE
    by_y = ((y + k) % SIDE) * SIDE + (x + m) % SIDE
    return jnp.where(lax.axis_index("fsdp") % 2 == 0, by_x, by_y)


def pack_kernel(wide, wanted, grads, mom, *refs):
    outs, terms, sems = refs[:-2], refs[-2], refs[-1]
    place = lax.axis_index("dp")
    per = wide // LANE
    cols = pl.ds(pl.multiple_of((place % per) * LANE, LANE), LANE)
    copies = []
    for i, (k, half) in enumerate(wanted):
        for m in range(SIDE):
            block = grads.at[0, matrix(k, m), :, pl.ds(half * wide, wide)]
            copies.append(pltpu.make_async_copy(block, outs[i].at[m], sems.at[0, i, m]))
            copies.append(pltpu.make_async_copy(mom.at[matrix(k, m)], terms.at[i, m], sems.at[1, i, m]))
    for copy in copies:
        copy.start()
    for copy in copies:
        copy.wait()
    for i, (_, half) in enumerate(wanted):

        @pl.when(place // per == half)
        def _():
            for m in range(SIDE):
                moment = MOMENTUM_DECAY * terms[i, m] + outs[i][m, :, cols].astype(F32)
                outs[i][m, :, cols] = moment.astype(BF16)


def pack(grads, momentum, wide, wanted, limit):
    rows = grads.shape[2]
    return pl.pallas_call(
        functools.partial(pack_kernel, wide, wanted),
        out_shape=(jax.ShapeDtypeStruct((SIDE, rows, wide), BF16),) * len(wanted),
        in_specs=[IN_HBM, IN_HBM],
        out_specs=(IN_VMEM,) * len(wanted),
        scratch_shapes=[
            pltpu.VMEM((len(wanted), SIDE, rows, LANE), F32),
            pltpu.SemaphoreType.DMA((2, len(wanted), SIDE)),
        ],
        compiler_params=pltpu.CompilerParams(vmem_limit_bytes=limit << 20),
        cost_estimate=cost(0, 4 * SIDE * rows * wide * len(wanted)),
    )(grads, momentum)


def add_kernel(count, split, *refs):
    inputs, outs = refs[: len(refs) - count[1]], refs[len(refs) - count[1] :]
    each = count[0]
    for place in range(len(inputs) // each):
        terms = inputs[place * each : (place + 1) * each]
        for m in range(SIDE):
            total = terms[0][m].astype(F32)
            for term in terms[1:]:
                total = total + term[m].astype(F32)
            if split:
                outs[place * SIDE + m][...] = total.astype(BF16)
            else:
                outs[place][m] = total.astype(BF16)


def add_up(groups, split):
    _, rows, wide = groups[0][0].shape
    if split:
        shape = (jax.ShapeDtypeStruct((rows, wide), BF16),) * (SIDE * len(groups))
    else:
        shape = (jax.ShapeDtypeStruct((SIDE, rows, wide), BF16),) * len(groups)
    inputs = [array for group in groups for array in group]
    return pl.pallas_call(
        functools.partial(add_kernel, (len(groups[0]), len(shape)), split),
        out_shape=shape,
        in_specs=[IN_VMEM] * len(inputs),
        out_specs=(IN_VMEM,) * len(shape),
        compiler_params=pltpu.CompilerParams(vmem_limit_bytes=16 << 20),
        cost_estimate=cost(0, 2 * SIDE * rows * wide * (len(inputs) + len(groups))),
    )(*inputs)


def combine_kernel(part0, part1, part2, part3, blocks, sent):
    for block in range(blocks.shape[0]):
        cols = slice(block * LANE, (block + 1) * LANE)
        total = part0[:, cols].astype(F32) + part1[:, cols].astype(F32)
        total = total + (part2[:, cols].astype(F32) + part3[:, cols].astype(F32))
        rounded = total.astype(BF16)
        blocks[block] = rounded
        sent[:, cols] = rounded


def combine(parts):
    rows, wide = parts[0].shape
    return pl.pallas_call(
        combine_kernel,
        out_shape=(
            jax.ShapeDtypeStruct((wide // LANE, rows, LANE), BF16),
            jax.ShapeDtypeStruct((rows, wide), BF16),
        ),
        in_specs=[IN_VMEM] * SIDE,
        out_specs=(IN_VMEM,) * 2,
        compiler_params=pltpu.CompilerParams(vmem_limit_bytes=16 << 20),
        cost_estimate=cost(0, 12 * rows * wide),
    )(*parts)


def gather(sent, core):
    rows, wide = sent.shape
    other = swap(sent)
    chip = jnp.concatenate([jnp.where(core == 0, sent, other), jnp.where(core == 0, other, sent)], axis=0)
    one = along_z(chip, 1)
    two = along_z(one, 1)
    three = along_z(two, 1)
    four = along_z(lax.dynamic_slice_in_dim(three, core * (wide // 2), wide // 2, axis=1), 1)
    return [chip, one, swap(one), two, swap(two), three, swap(three), four, swap(four)]


def fetch(groups, places, target, first, sems):
    core = lax.axis_index("fsdp") % 2
    copies = []
    for index, group in enumerate(groups):
        high, wide = group[0].shape[0], target.shape[1] // HALVES
        for piece, place in zip(group, places):
            row, width, start = min(place, RING - 1) * high, wide, index * wide
            if place >= RING - 1:
                width = wide // 2
                right = core if place == RING - 1 else 1 - core
                start = pl.multiple_of(start + right * width, LANE)
            into = target.at[pl.ds(row - first, high), pl.ds(start, width)]
            copies.append(pltpu.make_async_copy(piece, into, sems.at[index, place]))
    for copy in copies:
        copy.start()
    for copy in copies:
        copy.wait()


def gram_strips(rows, gram, start, stop):
    for at in range(start, stop, 256):
        end = min(at + 256, stop)
        term = lax.dot_general(
            rows[at:end, :], rows[0:end, :], ROWS_BY_ROWS, preferred_element_type=F32
        ).astype(BF16)
        gram[at:end, 0:end] = term
        if at:
            gram[0:at, at:end] = term[:, :at].T


def gram_kernel(places, start, stop, *refs):
    count = len(places)
    groups = [refs[count * i : count * (i + 1)] for i in range(HALVES)]
    rows, gram, sems = refs[-3:]
    fetch(groups, places, rows, 0, sems)
    gram_strips(rows, gram, start, stop)


def add_gram(groups, places, start, stop, before):
    high, wide = groups[0][0].shape
    size = RING * high
    pieces = [group[place] for group in groups for place in places]
    return pl.pallas_call(
        functools.partial(gram_kernel, places, start, stop),
        out_shape=(
            jax.ShapeDtypeStruct((size, HALVES * wide), BF16),
            jax.ShapeDtypeStruct((size, size), BF16),
        ),
        in_specs=[ANYWHERE] * len(pieces) + [IN_VMEM] * len(before),
        out_specs=(IN_VMEM,) * 2,
        scratch_shapes=[pltpu.SemaphoreType.DMA((HALVES, PIECES))],
        input_output_aliases={len(pieces) + i: i for i in range(len(before))},
        compiler_params=pltpu.CompilerParams(vmem_limit_bytes=24 << 20),
        cost_estimate=cost(2 * (stop - start) * stop * wide * HALVES, 2 * len(pieces) * high * wide),
    )(*pieces, *before)


def finish_kernel(places, start, *refs):
    count = len(places)
    groups = [refs[count * i : count * (i + 1)] for i in range(HALVES)]
    refs = refs[count * HALVES :]
    moments, (_, _, out, rows, gram, sems) = refs[:HALVES], refs[HALVES:]
    fetch(groups, places, rows, 0, sems)
    size, cols = rows.shape
    own = out.shape[2]
    block = 0
    for moment in moments:
        for i in range(moment.shape[0]):
            out[block, 0] = moment[i]
            block += 1
    gram_strips(rows, gram, start, size)
    total = jnp.zeros((1, 1), F32)
    for at in range(0, size, LANE):
        term = gram[at : at + LANE, at : at + LANE].astype(F32)
        here = lax.broadcasted_iota(jnp.int32, term.shape, 0)
        there = lax.broadcasted_iota(jnp.int32, term.shape, 1)
        total = total + jnp.sum(jnp.where(here == there, term, 0.0), keepdims=True)
    inverse = 1.0 / (jnp.sqrt(total) + EPS_NORM)

    def times_gram(value):
        value = (value * inverse).astype(BF16)
        return jnp.dot(value, gram[...], preferred_element_type=F32) * inverse

    def poly(times, value):
        once = times(value)
        twice = times(once)
        return COEF_A * value + COEF_B * once + COEF_C * twice

    first = (lax.axis_index("fsdp") % 2) * own
    unit = (
        lax.broadcasted_iota(jnp.int32, (own, size), 0) + first
        == lax.broadcasted_iota(jnp.int32, (own, size), 1)
    ).astype(F32)
    value = poly(times_gram, unit)
    value = poly(lambda v: poly(times_gram, times_gram(poly(times_gram, v))), value)
    high = jnp.where(total < jnp.inf, value * inverse, 0.0).astype(BF16)
    for at in range(0, cols, 512):
        result = jnp.dot(high, rows[:, at : at + 512], preferred_element_type=F32).astype(BF16)
        for col in range(0, 512, LANE):
            out[(at + col) // LANE, 1] = result[:, col : col + LANE]


def finish(groups, places, start, moments, before):
    high, wide = groups[0][0].shape
    size = RING * high
    own = moments[0].shape[1]
    cols = HALVES * wide
    pieces = [group[place] for group in groups for place in places]
    inputs = len(pieces) + len(moments)
    return pl.pallas_call(
        functools.partial(finish_kernel, places, start),
        out_shape=(
            jax.ShapeDtypeStruct((cols // LANE, 2, own, LANE), BF16),
            jax.ShapeDtypeStruct((size, cols), BF16),
            jax.ShapeDtypeStruct((size, size), BF16),
        ),
        in_specs=[ANYWHERE] * len(pieces) + [IN_VMEM] * (len(moments) + 2),
        out_specs=(IN_VMEM,) * 3,
        scratch_shapes=[pltpu.SemaphoreType.DMA((HALVES, PIECES))],
        input_output_aliases={inputs: 1, inputs + 1: 2},
        compiler_params=pltpu.CompilerParams(vmem_limit_bytes=32 << 20),
        cost_estimate=cost(26 * own * size * size + size * size * cols, 2 * size * (size + cols)),
    )(*pieces, *moments, *before)[0]


def update_kernel(scale, returned, weights, moment_new, new_weights, update):
    moment_new[...] = returned[:, 0].astype(F32)
    direction = scale * returned[:, 1].astype(F32)
    update[...] = direction.astype(BF16)
    kept = weights[...].astype(F32) * (1.0 - LEARN_RATE * DECAY_RATE)
    new_weights[...] = (kept - LEARN_RATE * direction).astype(BF16)


def apply_update(returned, weights, scale):
    shape = weights.shape
    return pl.pallas_call(
        functools.partial(update_kernel, scale),
        out_shape=(
            jax.ShapeDtypeStruct(shape, F32),
            jax.ShapeDtypeStruct(shape, BF16),
            jax.ShapeDtypeStruct(shape, BF16),
        ),
        in_specs=[IN_VMEM] * 2,
        out_specs=(IN_VMEM,) * 3,
        compiler_params=pltpu.CompilerParams(vmem_limit_bytes=16 << 20),
    )(returned, weights)


def body(grads, momentum, weights):
    _, rows_dev, cols_dev = momentum.shape
    rows_total = rows_dev * lax.axis_size("fsdp")
    cols_total = cols_dev * lax.axis_size("dp")
    wide = cols_total // HALVES
    core = lax.axis_index("fsdp") % 2
    up1, down1 = pack(grads, momentum, wide, ((2, 0), (2, 1)), 59)
    up1, down1 = first_hop(up1, 1), first_hop(down1, -1)
    up2, down2 = pack(grads, momentum, wide, ((1, 1), (3, 0)), 59)
    up2, down2 = first_hop(up2, 1), first_hop(down2, -1)
    next_up, next_down, own0, own1 = pack(
        grads, momentum, wide, ((1, 0), (3, 1), (0, 0), (0, 1)), 48
    )
    up3, down3 = add_up(((next_up, up1), (next_down, down1)), False)
    up3, down3 = first_hop(up3, 1), first_hop(down3, -1)

    sums = add_up(((own0, down2, up3), (own1, up2, down3)), True)
    moments, groups = [], []
    for half in range(HALVES):
        parts = sums[SIDE * half : SIDE * (half + 1)]
        parts = [parts[0]] + [second_hop(parts[k], k) for k in (1, 2, 3)]
        moment, sent = combine(parts)
        moments.append(moment)
        groups.append(gather(sent, core))
    size = rows_total
    bounds = (size * 6 // 11, size * 9 // 11)
    before = add_gram(groups, range(0, 5), 0, bounds[0], ())
    before = add_gram(groups, range(5, 7), bounds[0], bounds[1], before)
    current = finish(groups, range(7, 9), bounds[1], moments, before)
    returned = lax.all_to_all(current, "dp", split_axis=0, concat_axis=0, tiled=True)
    return apply_update(returned, weights, 0.2 * math.sqrt(max(rows_total, cols_total)))


def solution(mesh):
    placed = (P("dp", None, "fsdp", None), P(None, "fsdp", "dp"), P(None, "fsdp", "dp"))
    return jax.shard_map(
        body,
        mesh=mesh,
        in_specs=placed,
        out_specs=(P(None, "fsdp", "dp"), P(None, "fsdp", "dp"), P(None, "fsdp", "dp")),
        check_vma=False,
    )
```

```python
import functools
import math

import jax
import jax.numpy as jnp
from jax import lax
from jax.experimental import pallas as pl
from jax.experimental.pallas import tpu as pltpu
from jax.sharding import PartitionSpec as P

NS_ITERS = 2
SIDE = 4
RING = 8
PIECES = RING + 1
LANE = 128
HALVES = 2

MOMENTUM_DECAY = 0.95
LEARN_RATE = 0.02
DECAY_RATE = 0.1
COEF_A = 3.4445
COEF_B = -4.775
COEF_C = 2.0315
EPS_NORM = 1e-07
F32 = jnp.float32
BF16 = jnp.bfloat16
ROWS_BY_ROWS = (((1,), (1,)), ((), ()))
ANYWHERE = pl.BlockSpec(memory_space=pl.ANY)
IN_HBM = pl.BlockSpec(memory_space=pltpu.HBM)
IN_VMEM = pl.BlockSpec(memory_space=pltpu.VMEM)


def move(value, target):
    pairs = []
    for y in range(SIDE):
        for x in range(SIDE):
            for z in range(RING):
                for core in range(2):
                    ty, tx, tz, tc = target(y, x, z, core)
                    there = (((ty % SIDE) * SIDE + tx % SIDE) * RING + tz % RING) * 2 + tc % 2
                    pairs.append((((y * SIDE + x) * RING + z) * 2 + core, there))
    return lax.ppermute(value, ("dp", "fsdp"), pairs)


def first_hop(value, k):
    return move(value, lambda y, x, z, c: (y, x + k, z, c) if c == 0 else (y + k, x, z, c))


def second_hop(value, k):
    return move(value, lambda y, x, z, c: (y + k, x, z, c) if c == 0 else (y, x + k, z, c))


def along_z(value, k):
    return move(value, lambda y, x, z, c: (y, x, z + k, c) if c == 0 else (y, x, z - k, c))


def swap(value):
    return move(value, lambda y, x, z, c: (y, x, z, c + 1))


def cost(flops, size):
    return pl.CostEstimate(flops=flops, bytes_accessed=size, transcendentals=0)


def matrix(k, m):
    place = lax.axis_index("dp")
    y, x = place // SIDE, place % SIDE
    by_x = ((y + m) % SIDE) * SIDE + (x + k) % SIDE
    by_y = ((y + k) % SIDE) * SIDE + (x + m) % SIDE
    return jnp.where(lax.axis_index("fsdp") % 2 == 0, by_x, by_y)


def pack_kernel(wide, wanted, grads, mom, *refs):
    outs, terms, sems = refs[:-2], refs[-2], refs[-1]
    place = lax.axis_index("dp")
    per = wide // LANE
    cols = pl.ds(pl.multiple_of((place % per) * LANE, LANE), LANE)
    copies = []
    for i, (k, half) in enumerate(wanted):
        for m in range(SIDE):
            block = grads.at[0, matrix(k, m), :, pl.ds(half * wide, wide)]
            copies.append(pltpu.make_async_copy(block, outs[i].at[m], sems.at[0, i, m]))
            copies.append(pltpu.make_async_copy(mom.at[matrix(k, m)], terms.at[i, m], sems.at[1, i, m]))
    for copy in copies:
        copy.start()
    for copy in copies:
        copy.wait()
    for i, (_, half) in enumerate(wanted):

        @pl.when(place // per == half)
        def _():
            for m in range(SIDE):
                moment = MOMENTUM_DECAY * terms[i, m] + outs[i][m, :, cols].astype(F32)
                outs[i][m, :, cols] = moment.astype(BF16)


def pack(grads, momentum, wide, wanted, limit):
    rows = grads.shape[2]
    return pl.pallas_call(
        functools.partial(pack_kernel, wide, wanted),
        out_shape=(jax.ShapeDtypeStruct((SIDE, rows, wide), BF16),) * len(wanted),
        in_specs=[IN_HBM, IN_HBM],
        out_specs=(IN_VMEM,) * len(wanted),
        scratch_shapes=[
            pltpu.VMEM((len(wanted), SIDE, rows, LANE), F32),
            pltpu.SemaphoreType.DMA((2, len(wanted), SIDE)),
        ],
        compiler_params=pltpu.CompilerParams(vmem_limit_bytes=limit << 20),
        cost_estimate=cost(0, 4 * SIDE * rows * wide * len(wanted)),
    )(grads, momentum)


def add_kernel(count, split, *refs):
    inputs, outs = refs[: len(refs) - count[1]], refs[len(refs) - count[1] :]
    each = count[0]
    for place in range(len(inputs) // each):
        terms = inputs[place * each : (place + 1) * each]
        for m in range(SIDE):
            total = terms[0][m].astype(F32)
            for term in terms[1:]:
                total = total + term[m].astype(F32)
            if split:
                outs[place * SIDE + m][...] = total.astype(BF16)
            else:
                outs[place][m] = total.astype(BF16)


def add_up(groups, split):
    _, rows, wide = groups[0][0].shape
    if split:
        shape = (jax.ShapeDtypeStruct((rows, wide), BF16),) * (SIDE * len(groups))
    else:
        shape = (jax.ShapeDtypeStruct((SIDE, rows, wide), BF16),) * len(groups)
    inputs = [array for group in groups for array in group]
    return pl.pallas_call(
        functools.partial(add_kernel, (len(groups[0]), len(shape)), split),
        out_shape=shape,
        in_specs=[IN_VMEM] * len(inputs),
        out_specs=(IN_VMEM,) * len(shape),
        compiler_params=pltpu.CompilerParams(vmem_limit_bytes=16 << 20),
        cost_estimate=cost(0, 2 * SIDE * rows * wide * (len(inputs) + len(groups))),
    )(*inputs)


def combine_kernel(part0, part1, part2, part3, blocks, sent):
    for block in range(blocks.shape[0]):
        cols = slice(block * LANE, (block + 1) * LANE)
        total = part0[:, cols].astype(F32) + part1[:, cols].astype(F32)
        total = total + (part2[:, cols].astype(F32) + part3[:, cols].astype(F32))
        rounded = total.astype(BF16)
        blocks[block] = rounded
        sent[:, cols] = rounded


def combine(parts):
    rows, wide = parts[0].shape
    return pl.pallas_call(
        combine_kernel,
        out_shape=(
            jax.ShapeDtypeStruct((wide // LANE, rows, LANE), BF16),
            jax.ShapeDtypeStruct((rows, wide), BF16),
        ),
        in_specs=[IN_VMEM] * SIDE,
        out_specs=(IN_VMEM,) * 2,
        compiler_params=pltpu.CompilerParams(vmem_limit_bytes=16 << 20),
        cost_estimate=cost(0, 12 * rows * wide),
    )(*parts)


def gather(sent, core):
    wide = sent.shape[1]
    same = along_z(sent, 1)
    cross = move(sent, lambda y, x, z, c: (y, x, z - 1, 1) if c == 0 else (y, x, z + 1, 0))
    other = swap(sent)
    chip, one = (
        jnp.concatenate([jnp.where(core == 0, mine, theirs), jnp.where(core == 0, theirs, mine)], axis=0)
        for mine, theirs in ((sent, other), (same, cross))
    )
    two = along_z(one, 1)
    three = along_z(two, 1)
    four = along_z(lax.dynamic_slice_in_dim(three, core * (wide // 2), wide // 2, axis=1), 1)
    return [chip, one, swap(one), two, swap(two), three, swap(three), four]


def fetch(groups, places, target, sems):
    core = lax.axis_index("fsdp") % 2
    copies = [[] for _ in places]
    for index, group in enumerate(groups):
        high, wide = group[0].shape[0], target.shape[1] // HALVES
        for i, place in enumerate(places):
            row, width, start = min(place, RING - 1) * high, wide, index * wide
            if place >= RING - 1:
                width = wide // 2
                right = core if place == RING - 1 else 1 - core
                start = pl.multiple_of(start + right * width, LANE)
            into = target.at[pl.ds(row, high), pl.ds(start, width)]
            copies[i].append(pltpu.make_async_copy(group[i], into, sems.at[index, place]))
    for piece in copies:
        for copy in piece:
            copy.start()
    return copies


def wait(copies):
    for piece in copies:
        for copy in piece:
            copy.wait()


def gram_strip(rows, gram, at, end):
    term = lax.dot_general(
        rows[at:end, :], rows[0:end, :], ROWS_BY_ROWS, preferred_element_type=F32
    ).astype(BF16)
    gram[at:end, 0:end] = term
    if at:
        gram[0:at, at:end] = term[:, :at].T


def split(refs, places):
    count = len(places)
    return [refs[count * i : count * (i + 1)] for i in range(HALVES)], refs[count * HALVES :]


def gram_kernel(places, stop, *refs):
    groups, (rows, gram, zero, sems) = split(refs, places)
    wait(fetch(groups, places, rows, sems))
    for at in range(0, stop, 256):
        gram_strip(rows, gram, at, min(at + 256, stop))
    zero[...] = jnp.zeros(zero.shape, BF16)


def first_gram(groups, places, stop):
    high, wide = groups[0][0].shape
    size = RING * high
    pieces = [group[place] for group in groups for place in places]
    return pl.pallas_call(
        functools.partial(gram_kernel, places, stop),
        out_shape=(
            jax.ShapeDtypeStruct((size, HALVES * wide), BF16),
            jax.ShapeDtypeStruct((size, size), BF16),
            jax.ShapeDtypeStruct((high, wide // 2), BF16),
        ),
        in_specs=[ANYWHERE] * len(pieces),
        out_specs=(IN_VMEM,) * 3,
        scratch_shapes=[pltpu.SemaphoreType.DMA((HALVES, PIECES))],
        compiler_params=pltpu.CompilerParams(vmem_limit_bytes=24 << 20),
        cost_estimate=cost(stop * stop * wide * HALVES, 2 * len(pieces) * high * wide),
    )(*pieces)


def finish_kernel(places, start, *refs):
    groups, refs = split(refs, places)
    moments, (_, _, out, rows, gram, sems) = refs[:HALVES], refs[HALVES:]
    copies = fetch(groups, places, rows, sems)
    size, cols = rows.shape
    own = out.shape[2]
    for half, moment in enumerate(moments):
        for block in range(moment.shape[0]):
            out[half * moment.shape[0] + block, 0] = moment[block]
    wait(copies)
    for at in range(start, size, 256):
        gram_strip(rows, gram, at, min(at + 256, size))
    total = jnp.zeros((1, 1), F32)
    for at in range(0, size, LANE):
        term = gram[at : at + LANE, at : at + LANE].astype(F32)
        here = lax.broadcasted_iota(jnp.int32, term.shape, 0)
        there = lax.broadcasted_iota(jnp.int32, term.shape, 1)
        total = total + jnp.sum(jnp.where(here == there, term, 0.0), keepdims=True)
    inverse = 1.0 / (jnp.sqrt(total) + EPS_NORM)

    def times_gram(value):
        value = (value * inverse).astype(BF16)
        return jnp.dot(value, gram[...], preferred_element_type=F32) * inverse

    def poly(value, once):
        return COEF_A * value + COEF_B * once + COEF_C * times_gram(once)

    first = (lax.axis_index("fsdp") % 2) * own
    unit = (
        lax.broadcasted_iota(jnp.int32, (own, size), 0) + first
        == lax.broadcasted_iota(jnp.int32, (own, size), 1)
    ).astype(F32)
    chip = gram[0 : 2 * own, :].astype(F32)
    once = jnp.where(first == 0, chip[:own], chip[own:]) * inverse * inverse

    def squeeze(value):
        value = times_gram(poly(value, times_gram(value)))
        return poly(value, times_gram(value))

    value = poly(unit, once)
    once = squeeze(value)
    value = COEF_A * value + COEF_B * once + COEF_C * squeeze(once)
    high = jnp.where(total < jnp.inf, value * inverse, 0.0).astype(BF16)
    for at in range(0, cols, 512):
        result = jnp.dot(high, rows[:, at : at + 512], preferred_element_type=F32).astype(BF16)
        for col in range(0, 512, LANE):
            out[(at + col) // LANE, 1] = result[:, col : col + LANE]


def finish(groups, places, start, moments, before):
    high, wide = groups[0][0].shape
    size = RING * high
    own = moments[0].shape[1]
    cols = HALVES * wide
    pieces = [group[place] for group in groups for place in places]
    inputs = len(pieces) + len(moments)
    return pl.pallas_call(
        functools.partial(finish_kernel, places, start),
        out_shape=(
            jax.ShapeDtypeStruct((cols // LANE, 2, own, LANE), BF16),
            jax.ShapeDtypeStruct((size, cols), BF16),
            jax.ShapeDtypeStruct((size, size), BF16),
        ),
        in_specs=[ANYWHERE] * len(pieces) + [IN_VMEM] * (len(moments) + 2),
        out_specs=(IN_VMEM,) * 3,
        scratch_shapes=[pltpu.SemaphoreType.DMA((HALVES, PIECES))],
        input_output_aliases={inputs: 1, inputs + 1: 2},
        compiler_params=pltpu.CompilerParams(vmem_limit_bytes=32 << 20),
        cost_estimate=cost(26 * own * size * size + size * size * cols, 2 * size * (size + cols)),
    )(*pieces, *moments, *before)[0]


def update_kernel(scale, returned, weights, moment_new, new_weights, update):
    moment_new[...] = returned[:, 0].astype(F32)
    direction = scale * returned[:, 1].astype(F32)
    update[...] = direction.astype(BF16)
    kept = weights[...].astype(F32) * (1.0 - LEARN_RATE * DECAY_RATE)
    new_weights[...] = (kept - LEARN_RATE * direction).astype(BF16)


def apply_update(returned, weights, scale):
    shape = weights.shape
    return pl.pallas_call(
        functools.partial(update_kernel, scale),
        out_shape=(
            jax.ShapeDtypeStruct(shape, F32),
            jax.ShapeDtypeStruct(shape, BF16),
            jax.ShapeDtypeStruct(shape, BF16),
        ),
        in_specs=[IN_VMEM] * 2,
        out_specs=(IN_VMEM,) * 3,
        compiler_params=pltpu.CompilerParams(vmem_limit_bytes=16 << 20),
    )(returned, weights)


def body(grads, momentum, weights):
    _, rows_dev, cols_dev = momentum.shape
    rows_total = rows_dev * lax.axis_size("fsdp")
    cols_total = cols_dev * lax.axis_size("dp")
    wide = cols_total // HALVES
    core = lax.axis_index("fsdp") % 2
    up1, down1 = pack(grads, momentum, wide, ((2, 0), (2, 1)), 59)
    up1, down1 = first_hop(up1, 1), first_hop(down1, -1)
    up2, down2 = pack(grads, momentum, wide, ((1, 1), (3, 0)), 59)
    up2, down2 = first_hop(up2, 1), first_hop(down2, -1)
    next_up, next_down, own0, own1 = pack(
        grads, momentum, wide, ((1, 0), (3, 1), (0, 0), (0, 1)), 48
    )
    up3, down3 = add_up(((next_up, up1), (next_down, down1)), False)
    up3, down3 = first_hop(up3, 1), first_hop(down3, -1)

    sums = add_up(((own0, down2, up3), (own1, up2, down3)), True)
    moments, groups = [], []
    for half in range(HALVES):
        parts = sums[SIDE * half : SIDE * (half + 1)]
        moment, sent = combine([parts[0]] + [second_hop(parts[k], k) for k in (1, 2, 3)])
        moments.append(moment)
        groups.append(gather(sent, core))
    stop = rows_total * 9 // 11
    *before, zero = first_gram(groups, range(0, 7), stop)
    for group in groups:
        group.append(swap(group[7] + zero))
    current = finish(groups, range(7, 9), stop, moments, before)
    returned = lax.all_to_all(current, "dp", split_axis=0, concat_axis=0, tiled=True)
    return apply_update(returned, weights, 0.2 * math.sqrt(max(rows_total, cols_total)))


def solution(mesh):
    placed = (P("dp", None, "fsdp", None), P(None, "fsdp", "dp"), P(None, "fsdp", "dp"))
    return jax.shard_map(
        body,
        mesh=mesh,
        in_specs=placed,
        out_specs=(P(None, "fsdp", "dp"), P(None, "fsdp", "dp"), P(None, "fsdp", "dp")),
        check_vma=False,
    )
```

```python
import functools
import math

import jax
import jax.numpy as jnp
from jax import lax
from jax.experimental import pallas as pl
from jax.experimental.pallas import tpu as pltpu
from jax.sharding import PartitionSpec as P

NS_ITERS = 2
SIDE = 4
RING = 8
PIECES = RING + 1
LANE = 128
HALVES = 2

MOMENTUM_DECAY = 0.95
LEARN_RATE = 0.02
DECAY_RATE = 0.1
COEF_A = 3.4445
COEF_B = -4.775
COEF_C = 2.0315
EPS_NORM = 1e-07
F32 = jnp.float32
BF16 = jnp.bfloat16
ROWS_BY_ROWS = (((1,), (1,)), ((), ()))
ANYWHERE = pl.BlockSpec(memory_space=pl.ANY)
IN_HBM = pl.BlockSpec(memory_space=pltpu.HBM)
IN_VMEM = pl.BlockSpec(memory_space=pltpu.VMEM)


def move(value, target):
    pairs = []
    for y in range(SIDE):
        for x in range(SIDE):
            for z in range(RING):
                for core in range(2):
                    ty, tx, tz, tc = target(y, x, z, core)
                    there = (((ty % SIDE) * SIDE + tx % SIDE) * RING + tz % RING) * 2 + tc % 2
                    pairs.append((((y * SIDE + x) * RING + z) * 2 + core, there))
    return lax.ppermute(value, ("dp", "fsdp"), pairs)


def first_hop(value, k):
    return move(value, lambda y, x, z, c: (y, x + k, z, c) if c == 0 else (y + k, x, z, c))


def second_hop(value, k):
    return move(value, lambda y, x, z, c: (y + k, x, z, c) if c == 0 else (y, x + k, z, c))


def along_z(value, k):
    return move(value, lambda y, x, z, c: (y, x, z + k, c) if c == 0 else (y, x, z - k, c))


def swap(value):
    return move(value, lambda y, x, z, c: (y, x, z, c + 1))


def cost(flops, size):
    return pl.CostEstimate(flops=flops, bytes_accessed=size, transcendentals=0)


def matrix(k, m):
    place = lax.axis_index("dp")
    y, x = place // SIDE, place % SIDE
    by_x = ((y + m) % SIDE) * SIDE + (x + k) % SIDE
    by_y = ((y + k) % SIDE) * SIDE + (x + m) % SIDE
    return jnp.where(lax.axis_index("fsdp") % 2 == 0, by_x, by_y)


def pack_kernel(wide, wanted, grads, mom, *refs):
    outs, terms, sems = refs[:-2], refs[-2], refs[-1]
    place = lax.axis_index("dp")
    per = wide // LANE
    cols = pl.ds(pl.multiple_of((place % per) * LANE, LANE), LANE)
    copies = []
    for i, (k, half) in enumerate(wanted):
        for m in range(SIDE):
            block = grads.at[0, matrix(k, m), :, pl.ds(half * wide, wide)]
            copies.append(pltpu.make_async_copy(block, outs[i].at[m], sems.at[0, i, m]))
            copies.append(pltpu.make_async_copy(mom.at[matrix(k, m)], terms.at[i, m], sems.at[1, i, m]))
    for copy in copies:
        copy.start()
    for copy in copies:
        copy.wait()
    for i, (_, half) in enumerate(wanted):

        @pl.when(place // per == half)
        def _():
            for m in range(SIDE):
                moment = MOMENTUM_DECAY * terms[i, m] + outs[i][m, :, cols].astype(F32)
                outs[i][m, :, cols] = moment.astype(BF16)


def pack(grads, momentum, wide, wanted, limit):
    rows = grads.shape[2]
    return pl.pallas_call(
        functools.partial(pack_kernel, wide, wanted),
        out_shape=(jax.ShapeDtypeStruct((SIDE, rows, wide), BF16),) * len(wanted),
        in_specs=[IN_HBM, IN_HBM],
        out_specs=(IN_VMEM,) * len(wanted),
        scratch_shapes=[
            pltpu.VMEM((len(wanted), SIDE, rows, LANE), F32),
            pltpu.SemaphoreType.DMA((2, len(wanted), SIDE)),
        ],
        compiler_params=pltpu.CompilerParams(vmem_limit_bytes=limit << 20),
        cost_estimate=cost(0, 4 * SIDE * rows * wide * len(wanted)),
    )(grads, momentum)


def add_kernel(count, split, *refs):
    inputs, outs = refs[: len(refs) - count[1]], refs[len(refs) - count[1] :]
    each = count[0]
    for place in range(len(inputs) // each):
        terms = inputs[place * each : (place + 1) * each]
        for m in range(SIDE):
            total = terms[0][m].astype(F32)
            for term in terms[1:]:
                total = total + term[m].astype(F32)
            if split:
                outs[place * SIDE + m][...] = total.astype(BF16)
            else:
                outs[place][m] = total.astype(BF16)


def add_up(groups, split):
    _, rows, wide = groups[0][0].shape
    if split:
        shape = (jax.ShapeDtypeStruct((rows, wide), BF16),) * (SIDE * len(groups))
    else:
        shape = (jax.ShapeDtypeStruct((SIDE, rows, wide), BF16),) * len(groups)
    inputs = [array for group in groups for array in group]
    return pl.pallas_call(
        functools.partial(add_kernel, (len(groups[0]), len(shape)), split),
        out_shape=shape,
        in_specs=[IN_VMEM] * len(inputs),
        out_specs=(IN_VMEM,) * len(shape),
        compiler_params=pltpu.CompilerParams(vmem_limit_bytes=16 << 20),
        cost_estimate=cost(0, 2 * SIDE * rows * wide * (len(inputs) + len(groups))),
    )(*inputs)


def combine_kernel(part0, part1, part2, part3, blocks, sent):
    for block in range(blocks.shape[0]):
        cols = slice(block * LANE, (block + 1) * LANE)
        total = part0[:, cols].astype(F32) + part1[:, cols].astype(F32)
        total = total + (part2[:, cols].astype(F32) + part3[:, cols].astype(F32))
        rounded = total.astype(BF16)
        blocks[block] = rounded
        sent[:, cols] = rounded


def combine(parts):
    rows, wide = parts[0].shape
    return pl.pallas_call(
        combine_kernel,
        out_shape=(
            jax.ShapeDtypeStruct((wide // LANE, rows, LANE), BF16),
            jax.ShapeDtypeStruct((rows, wide), BF16),
        ),
        in_specs=[IN_VMEM] * SIDE,
        out_specs=(IN_VMEM,) * 2,
        compiler_params=pltpu.CompilerParams(vmem_limit_bytes=16 << 20),
        cost_estimate=cost(0, 12 * rows * wide),
    )(*parts)


def gather(sent, core, whole):
    wide = sent.shape[1]
    same = along_z(sent, 1)
    cross = move(sent, lambda y, x, z, c: (y, x, z - 1, 1) if c == 0 else (y, x, z + 1, 0))
    other = swap(sent)
    chip, one = (
        jnp.concatenate([jnp.where(core == 0, mine, theirs), jnp.where(core == 0, theirs, mine)], axis=0)
        for mine, theirs in ((sent, other), (same, cross))
    )
    two = along_z(one, 1)
    three = along_z(two, 1)
    last = three
    if not whole:
        last = lax.dynamic_slice_in_dim(three, core * (wide // 2), wide // 2, axis=1)
    return [chip, one, swap(one), two, swap(two), three, swap(three), along_z(last, 1)]


def fetch(groups, begin, target, sems):
    core = lax.axis_index("fsdp") % 2
    copies = []
    for index, group in enumerate(groups):
        high, wide = group[0].shape[0], target.shape[1] // HALVES
        for place, piece in enumerate(group, begin):
            row, width, start = min(place, RING - 1) * high, piece.shape[1], index * wide
            if width < wide:
                right = core if place == RING - 1 else 1 - core
                start = pl.multiple_of(start + right * width, LANE)
            into = target.at[pl.ds(row, high), pl.ds(start, width)]
            copies.append(pltpu.make_async_copy(piece, into, sems.at[index, place]))
    for copy in copies:
        copy.start()
    return copies


def wait(copies):
    for copy in copies:
        copy.wait()


def gram_strip(rows, gram, at, end):
    term = lax.dot_general(
        rows[at:end, :], rows[0:end, :], ROWS_BY_ROWS, preferred_element_type=F32
    ).astype(BF16)
    gram[at:end, 0:end] = term
    if at:
        gram[0:at, at:end] = term[:, :at].T


def split(refs, counts):
    first, second = counts
    return (refs[:first], refs[first : first + second]), refs[first + second :]


def gram_kernel(counts, stop, *refs):
    groups, (rows, gram, zero, sems) = split(refs, counts)
    wait(fetch(groups, 0, rows, sems))
    for at in range(0, stop, 256):
        gram_strip(rows, gram, at, min(at + 256, stop))
    zero[...] = jnp.zeros(zero.shape, BF16)


def first_gram(groups, stop):
    high, wide = groups[0][0].shape
    size = RING * high
    pieces = [piece for group in groups for piece in group]
    return pl.pallas_call(
        functools.partial(gram_kernel, [len(group) for group in groups], stop),
        out_shape=(
            jax.ShapeDtypeStruct((size, HALVES * wide), BF16),
            jax.ShapeDtypeStruct((size, size), BF16),
            jax.ShapeDtypeStruct((high, wide // 2), BF16),
        ),
        in_specs=[ANYWHERE] * len(pieces),
        out_specs=(IN_VMEM,) * 3,
        scratch_shapes=[pltpu.SemaphoreType.DMA((HALVES, PIECES))],
        compiler_params=pltpu.CompilerParams(vmem_limit_bytes=24 << 20),
        cost_estimate=cost(stop * stop * wide * HALVES, 2 * len(pieces) * high * wide),
    )(*pieces)


def finish_kernel(counts, start, *refs):
    groups, refs = split(refs, counts)
    moments, (_, _, out, rows, gram, sems) = refs[:HALVES], refs[HALVES:]
    copies = fetch(groups, RING - 1, rows, sems)
    size, cols = rows.shape
    own = out.shape[2]
    for half, moment in enumerate(moments):
        for block in range(moment.shape[0]):
            out[half * moment.shape[0] + block, 0] = moment[block]
    wait(copies)
    for at in range(start, size, 256):
        gram_strip(rows, gram, at, min(at + 256, size))
    total = jnp.zeros((1, 1), F32)
    for at in range(0, size, LANE):
        term = gram[at : at + LANE, at : at + LANE].astype(F32)
        here = lax.broadcasted_iota(jnp.int32, term.shape, 0)
        there = lax.broadcasted_iota(jnp.int32, term.shape, 1)
        total = total + jnp.sum(jnp.where(here == there, term, 0.0), keepdims=True)
    inverse = 1.0 / (jnp.sqrt(total) + EPS_NORM)

    first = (lax.axis_index("fsdp") % 2) * own
    chip = gram[0 : 2 * own, :].astype(F32)
    gram_rows = jnp.where(first == 0, chip[:own], chip[own:]) * inverse * inverse

    def times_gram(scalar, rest):
        product = (rest * inverse).astype(BF16)
        product = jnp.dot(product, gram[...], preferred_element_type=F32) * inverse
        return product + scalar * gram_rows if scalar else product

    def poly(scalar, rest, once):
        return COEF_A * scalar, COEF_A * rest + COEF_B * once + COEF_C * times_gram(0.0, once)

    def squeeze(scalar, rest):
        scalar, rest = poly(scalar, rest, times_gram(scalar, rest))
        rest = times_gram(scalar, rest)
        return poly(0.0, rest, times_gram(0.0, rest))[1]

    scalar, rest = poly(1.0, 0.0, gram_rows)
    once = squeeze(scalar, rest)
    rest = COEF_A * rest + COEF_B * once + COEF_C * squeeze(0.0, once)
    scalar = COEF_A * scalar
    finite = total < jnp.inf
    high = jnp.where(finite, rest * inverse, 0.0).astype(BF16)
    scalar = jnp.where(finite, scalar * inverse, 0.0)
    chip_rows = rows[0 : 2 * own, :].astype(F32)
    own_rows = jnp.where(first == 0, chip_rows[:own], chip_rows[own:])
    for at in range(0, cols, 512):
        result = jnp.dot(high, rows[:, at : at + 512], preferred_element_type=F32)
        result = (result + scalar * own_rows[:, at : at + 512]).astype(BF16)
        for col in range(0, 512, LANE):
            out[(at + col) // LANE, 1] = result[:, col : col + LANE]


def finish(groups, start, moments, before):
    size, cols = before[0].shape
    own = moments[0].shape[1]
    pieces = [piece for group in groups for piece in group]
    inputs = len(pieces) + len(moments)
    return pl.pallas_call(
        functools.partial(finish_kernel, [len(group) for group in groups], start),
        out_shape=(
            jax.ShapeDtypeStruct((cols // LANE, 2, own, LANE), BF16),
            jax.ShapeDtypeStruct((size, cols), BF16),
            jax.ShapeDtypeStruct((size, size), BF16),
        ),
        in_specs=[ANYWHERE] * len(pieces) + [IN_VMEM] * (len(moments) + 2),
        out_specs=(IN_VMEM,) * 3,
        scratch_shapes=[pltpu.SemaphoreType.DMA((HALVES, PIECES))],
        input_output_aliases={inputs: 1, inputs + 1: 2},
        compiler_params=pltpu.CompilerParams(vmem_limit_bytes=32 << 20),
        cost_estimate=cost(26 * own * size * size + size * size * cols, 2 * size * (size + cols)),
    )(*pieces, *moments, *before)[0]


def update_kernel(scale, returned, weights, moment_new, new_weights, update):
    moment_new[...] = returned[:, 0].astype(F32)
    direction = scale * returned[:, 1].astype(F32)
    update[...] = direction.astype(BF16)
    kept = weights[...].astype(F32) * (1.0 - LEARN_RATE * DECAY_RATE)
    new_weights[...] = (kept - LEARN_RATE * direction).astype(BF16)


def apply_update(returned, weights, scale):
    shape = weights.shape
    return pl.pallas_call(
        functools.partial(update_kernel, scale),
        out_shape=(
            jax.ShapeDtypeStruct(shape, F32),
            jax.ShapeDtypeStruct(shape, BF16),
            jax.ShapeDtypeStruct(shape, BF16),
        ),
        in_specs=[IN_VMEM] * 2,
        out_specs=(IN_VMEM,) * 3,
        compiler_params=pltpu.CompilerParams(vmem_limit_bytes=16 << 20),
    )(returned, weights)


def body(grads, momentum, weights):
    _, rows_dev, cols_dev = momentum.shape
    rows_total = rows_dev * lax.axis_size("fsdp")
    cols_total = cols_dev * lax.axis_size("dp")
    wide = cols_total // HALVES
    core = lax.axis_index("fsdp") % 2
    up1, down1 = pack(grads, momentum, wide, ((2, 0), (2, 1)), 59)
    up1, down1 = first_hop(up1, 1), first_hop(down1, -1)
    up2, down2 = pack(grads, momentum, wide, ((1, 1), (3, 0)), 59)
    up2, down2 = first_hop(up2, 1), first_hop(down2, -1)
    next_up, next_down, own0, own1 = pack(
        grads, momentum, wide, ((1, 0), (3, 1), (0, 0), (0, 1)), 48
    )
    up3, down3 = add_up(((next_up, up1), (next_down, down1)), False)
    up3, down3 = first_hop(up3, 1), first_hop(down3, -1)

    sums = add_up(((own0, down2, up3), (own1, up2, down3)), True)
    moments, groups = [], []
    for half in range(HALVES):
        parts = sums[SIDE * half : SIDE * (half + 1)]
        moment, sent = combine([parts[0]] + [second_hop(parts[k], k) for k in (1, 2, 3)])
        moments.append(moment)
        groups.append(gather(sent, core, half == 0))
    stop = rows_total * 9 // 11
    *before, zero = first_gram([groups[0][: RING - 1], groups[1][: RING - 1]], stop)
    last = groups[1][RING - 1]
    ends = [groups[0][RING - 1 :], [last, swap(last + zero)]]
    current = finish(ends, stop, moments, before)
    returned = lax.all_to_all(current, "dp", split_axis=0, concat_axis=0, tiled=True)
    return apply_update(returned, weights, 0.2 * math.sqrt(max(rows_total, cols_total)))


def solution(mesh):
    placed = (P("dp", None, "fsdp", None), P(None, "fsdp", "dp"), P(None, "fsdp", "dp"))
    return jax.shard_map(
        body,
        mesh=mesh,
        in_specs=placed,
        out_specs=(P(None, "fsdp", "dp"), P(None, "fsdp", "dp"), P(None, "fsdp", "dp")),
        check_vma=False,
    )
```

```python
import functools
import math

import jax
import jax.numpy as jnp
from jax import lax
from jax.experimental import pallas as pl
from jax.experimental.pallas import tpu as pltpu
from jax.sharding import PartitionSpec as P

SIDE = 4
RING = 8
PIECES = RING + 1
LANE = 128
HALVES = 2

MOMENTUM_DECAY = 0.95
LEARN_RATE = 0.02
DECAY_RATE = 0.1
COEF_A = 3.4445
COEF_B = -4.775
COEF_C = 2.0315
EPS_NORM = 1e-07
F32 = jnp.float32
BF16 = jnp.bfloat16
ROWS_BY_ROWS = (((1,), (1,)), ((), ()))
ANYWHERE = pl.BlockSpec(memory_space=pl.ANY)
IN_HBM = pl.BlockSpec(memory_space=pltpu.HBM)
IN_VMEM = pl.BlockSpec(memory_space=pltpu.VMEM)


def move(value, target):
    pairs = []
    for y in range(SIDE):
        for x in range(SIDE):
            for z in range(RING):
                for core in range(2):
                    ty, tx, tz, tc = target(y, x, z, core)
                    there = (((ty % SIDE) * SIDE + tx % SIDE) * RING + tz % RING) * 2 + tc % 2
                    pairs.append((((y * SIDE + x) * RING + z) * 2 + core, there))
    return lax.ppermute(value, ("dp", "fsdp"), pairs)


def first_hop(value, k):
    return move(value, lambda y, x, z, c: (y, x + k, z, c) if c == 0 else (y + k, x, z, c))


def second_hop(value, k):
    return move(value, lambda y, x, z, c: (y + k, x, z, c) if c == 0 else (y, x + k, z, c))


def along_z(value, k):
    return move(value, lambda y, x, z, c: (y, x, z + k, c) if c == 0 else (y, x, z - k, c))


def swap(value):
    return move(value, lambda y, x, z, c: (y, x, z, c + 1))


def cost(flops, size):
    return pl.CostEstimate(flops=flops, bytes_accessed=size, transcendentals=0)


def matrix(k, m):
    place = lax.axis_index("dp")
    y, x = place // SIDE, place % SIDE
    by_x = ((y + m) % SIDE) * SIDE + (x + k) % SIDE
    by_y = ((y + k) % SIDE) * SIDE + (x + m) % SIDE
    return jnp.where(lax.axis_index("fsdp") % 2 == 0, by_x, by_y)


def pack_kernel(wide, wanted, grads, mom, *refs):
    outs, terms, sems = refs[:-2], refs[-2], refs[-1]
    place = lax.axis_index("dp")
    per = wide // LANE
    cols = pl.ds(pl.multiple_of((place % per) * LANE, LANE), LANE)
    copies = []
    for i, (k, half) in enumerate(wanted):
        for m in range(SIDE):
            block = grads.at[0, matrix(k, m), :, pl.ds(half * wide, wide)]
            copies.append(pltpu.make_async_copy(block, outs[i].at[m], sems.at[0, i, m]))
            copies.append(pltpu.make_async_copy(mom.at[matrix(k, m)], terms.at[i, m], sems.at[1, i, m]))
    for copy in copies:
        copy.start()
    for copy in copies:
        copy.wait()
    for i, (_, half) in enumerate(wanted):

        @pl.when(place // per == half)
        def _():
            for m in range(SIDE):
                moment = MOMENTUM_DECAY * terms[i, m] + outs[i][m, :, cols].astype(F32)
                outs[i][m, :, cols] = moment.astype(BF16)


def pack(grads, momentum, wide, wanted, limit):
    rows = grads.shape[2]
    return pl.pallas_call(
        functools.partial(pack_kernel, wide, wanted),
        out_shape=(jax.ShapeDtypeStruct((SIDE, rows, wide), BF16),) * len(wanted),
        in_specs=[IN_HBM, IN_HBM],
        out_specs=(IN_VMEM,) * len(wanted),
        scratch_shapes=[
            pltpu.VMEM((len(wanted), SIDE, rows, LANE), F32),
            pltpu.SemaphoreType.DMA((2, len(wanted), SIDE)),
        ],
        compiler_params=pltpu.CompilerParams(vmem_limit_bytes=limit << 20),
        cost_estimate=cost(0, 4 * SIDE * rows * wide * len(wanted)),
    )(grads, momentum)


def add_kernel(count, split, *refs):
    inputs, outs = refs[: len(refs) - count[1]], refs[len(refs) - count[1] :]
    each = count[0]
    for place in range(len(inputs) // each):
        terms = inputs[place * each : (place + 1) * each]
        for m in range(SIDE):
            total = terms[0][m].astype(F32)
            for term in terms[1:]:
                total = total + term[m].astype(F32)
            if split:
                outs[place * SIDE + m][...] = total.astype(BF16)
            else:
                outs[place][m] = total.astype(BF16)


def add_up(groups, split):
    _, rows, wide = groups[0][0].shape
    if split:
        shape = (jax.ShapeDtypeStruct((rows, wide), BF16),) * (SIDE * len(groups))
    else:
        shape = (jax.ShapeDtypeStruct((SIDE, rows, wide), BF16),) * len(groups)
    inputs = [array for group in groups for array in group]
    return pl.pallas_call(
        functools.partial(add_kernel, (len(groups[0]), len(shape)), split),
        out_shape=shape,
        in_specs=[IN_VMEM] * len(inputs),
        out_specs=(IN_VMEM,) * len(shape),
        compiler_params=pltpu.CompilerParams(vmem_limit_bytes=16 << 20),
        cost_estimate=cost(0, 2 * SIDE * rows * wide * (len(inputs) + len(groups))),
    )(*inputs)


def combine_kernel(part0, part1, part2, part3, blocks, sent):
    for block in range(blocks.shape[0]):
        cols = slice(block * LANE, (block + 1) * LANE)
        total = part0[:, cols].astype(F32) + part1[:, cols].astype(F32)
        total = total + (part2[:, cols].astype(F32) + part3[:, cols].astype(F32))
        rounded = total.astype(BF16)
        blocks[block] = rounded
        sent[:, cols] = rounded


def combine(parts):
    rows, wide = parts[0].shape
    return pl.pallas_call(
        combine_kernel,
        out_shape=(
            jax.ShapeDtypeStruct((wide // LANE, rows, LANE), BF16),
            jax.ShapeDtypeStruct((rows, wide), BF16),
        ),
        in_specs=[IN_VMEM] * SIDE,
        out_specs=(IN_VMEM,) * 2,
        compiler_params=pltpu.CompilerParams(vmem_limit_bytes=16 << 20),
        cost_estimate=cost(0, 12 * rows * wide),
    )(*parts)


def gather(sent, core, whole):
    wide = sent.shape[1]
    same = along_z(sent, 1)
    cross = move(sent, lambda y, x, z, c: (y, x, z - 1, 1) if c == 0 else (y, x, z + 1, 0))
    other = swap(sent)
    chip, one = (
        jnp.concatenate([jnp.where(core == 0, mine, theirs), jnp.where(core == 0, theirs, mine)], axis=0)
        for mine, theirs in ((sent, other), (same, cross))
    )
    two = along_z(one, 1)
    three = along_z(two, 1)
    last = three
    if not whole:
        last = lax.dynamic_slice_in_dim(three, core * (wide // 2), wide // 2, axis=1)
    return [chip, one, swap(one), two, swap(two), three, swap(three), along_z(last, 1)]


def fetch(groups, begin, target, sems):
    core = lax.axis_index("fsdp") % 2
    copies = []
    for index, group in enumerate(groups):
        high, wide = group[0].shape[0], target.shape[1] // HALVES
        for place, piece in enumerate(group, begin):
            row, width, start = min(place, RING - 1) * high, piece.shape[1], index * wide
            if width < wide:
                right = core if place == RING - 1 else 1 - core
                start = pl.multiple_of(start + right * width, LANE)
            into = target.at[pl.ds(row, high), pl.ds(start, width)]
            copies.append(pltpu.make_async_copy(piece, into, sems.at[index, place]))
    for copy in copies:
        copy.start()
    return copies


def wait(copies):
    for copy in copies:
        copy.wait()


def gram_strip(rows, gram, at, end):
    term = lax.dot_general(
        rows[at:end, :], rows[0:end, :], ROWS_BY_ROWS, preferred_element_type=F32
    ).astype(BF16)
    gram[at:end, 0:end] = term
    if at:
        gram[0:at, at:end] = term[:, :at].T


def split(refs, counts):
    first, second = counts
    return (refs[:first], refs[first : first + second]), refs[first + second :]


def gram_kernel(counts, stop, *refs):
    groups, (rows, gram, zero, sems) = split(refs, counts)
    wait(fetch(groups, 0, rows, sems))
    for at in range(0, stop, 256):
        gram_strip(rows, gram, at, min(at + 256, stop))
    zero[...] = jnp.zeros(zero.shape, BF16)


def first_gram(groups, stop):
    high, wide = groups[0][0].shape
    size = RING * high
    pieces = [piece for group in groups for piece in group]
    return pl.pallas_call(
        functools.partial(gram_kernel, [len(group) for group in groups], stop),
        out_shape=(
            jax.ShapeDtypeStruct((size, HALVES * wide), BF16),
            jax.ShapeDtypeStruct((size, size), BF16),
            jax.ShapeDtypeStruct((high, wide // 2), BF16),
        ),
        in_specs=[ANYWHERE] * len(pieces),
        out_specs=(IN_VMEM,) * 3,
        scratch_shapes=[pltpu.SemaphoreType.DMA((HALVES, PIECES))],
        compiler_params=pltpu.CompilerParams(vmem_limit_bytes=24 << 20),
        cost_estimate=cost(stop * stop * wide * HALVES, 2 * len(pieces) * high * wide),
    )(*pieces)


def finish_kernel(counts, start, *refs):
    groups, refs = split(refs, counts)
    moments, (_, _, out, rows, gram, current, result, sems) = refs[:HALVES], refs[HALVES:]
    copies = fetch(groups, RING - 1, rows, sems)
    size, cols = rows.shape
    own = out.shape[2]
    for half, moment in enumerate(moments):
        for block in range(moment.shape[0]):
            out[half * moment.shape[0] + block, 0] = moment[block]
    wait(copies)
    for at in range(start, size, 256):
        gram_strip(rows, gram, at, min(at + 256, size))
    total = jnp.zeros((1, 1), F32)
    for at in range(0, size, LANE):
        term = gram[at : at + LANE, at : at + LANE].astype(F32)
        here = lax.broadcasted_iota(jnp.int32, term.shape, 0)
        there = lax.broadcasted_iota(jnp.int32, term.shape, 1)
        total = total + jnp.sum(jnp.where(here == there, term, 0.0), keepdims=True)
    inverse = 1.0 / (jnp.sqrt(total) + EPS_NORM)

    first = (lax.axis_index("fsdp") % 2) * own
    chip = gram[0 : 2 * own, :].astype(F32)
    gram_rows = jnp.where(first == 0, chip[:own], chip[own:]) * inverse * inverse

    def times_gram(rest):
        rest = (rest * inverse).astype(BF16)
        return jnp.dot(rest, gram[...], preferred_element_type=F32) * inverse

    current[...] = COEF_B * gram_rows + COEF_C * times_gram(gram_rows)
    result[...] = COEF_A * current[...]

    @pl.loop(0, 2)
    def _(step):
        scalar = jnp.where(step == 0, COEF_A, 0.0)
        once = times_gram(current[...]) + scalar * gram_rows
        current[...] = COEF_A * current[...] + COEF_B * once + COEF_C * times_gram(once)
        value = times_gram(current[...]) + COEF_A * scalar * gram_rows
        once = times_gram(value)
        value = COEF_A * value + COEF_B * once + COEF_C * times_gram(once)
        result[...] += jnp.where(step == 0, COEF_B, COEF_C) * value
        current[...] = value

    rest = result[...]
    scalar = COEF_A * COEF_A
    finite = total < jnp.inf
    high = jnp.where(finite, rest * inverse, 0.0).astype(BF16)
    scalar = jnp.where(finite, scalar * inverse, 0.0)
    chip_rows = rows[0 : 2 * own, :].astype(F32)
    own_rows = jnp.where(first == 0, chip_rows[:own], chip_rows[own:])
    for at in range(0, cols, 512):
        term = jnp.dot(high, rows[:, at : at + 512], preferred_element_type=F32)
        term = (term + scalar * own_rows[:, at : at + 512]).astype(BF16)
        for col in range(0, 512, LANE):
            out[(at + col) // LANE, 1] = term[:, col : col + LANE]


def finish(groups, start, moments, before):
    size, cols = before[0].shape
    own = moments[0].shape[1]
    pieces = [piece for group in groups for piece in group]
    inputs = len(pieces) + len(moments)
    return pl.pallas_call(
        functools.partial(finish_kernel, [len(group) for group in groups], start),
        out_shape=(
            jax.ShapeDtypeStruct((cols // LANE, 2, own, LANE), BF16),
            jax.ShapeDtypeStruct((size, cols), BF16),
            jax.ShapeDtypeStruct((size, size), BF16),
        ),
        in_specs=[ANYWHERE] * len(pieces) + [IN_VMEM] * (len(moments) + 2),
        out_specs=(IN_VMEM,) * 3,
        scratch_shapes=[
            pltpu.VMEM((own, size), F32),
            pltpu.VMEM((own, size), F32),
            pltpu.SemaphoreType.DMA((HALVES, PIECES)),
        ],
        input_output_aliases={inputs: 1, inputs + 1: 2},
        compiler_params=pltpu.CompilerParams(vmem_limit_bytes=32 << 20),
        cost_estimate=cost(26 * own * size * size + size * size * cols, 2 * size * (size + cols)),
    )(*pieces, *moments, *before)[0]


def update_kernel(scale, returned, weights, moment_new, new_weights, update):
    moment_new[...] = returned[:, 0].astype(F32)
    direction = scale * returned[:, 1].astype(F32)
    update[...] = direction.astype(BF16)
    kept = weights[...].astype(F32) * (1.0 - LEARN_RATE * DECAY_RATE)
    new_weights[...] = (kept - LEARN_RATE * direction).astype(BF16)


def apply_update(returned, weights, scale):
    shape = weights.shape
    return pl.pallas_call(
        functools.partial(update_kernel, scale),
        out_shape=(
            jax.ShapeDtypeStruct(shape, F32),
            jax.ShapeDtypeStruct(shape, BF16),
            jax.ShapeDtypeStruct(shape, BF16),
        ),
        in_specs=[IN_VMEM] * 2,
        out_specs=(IN_VMEM,) * 3,
        compiler_params=pltpu.CompilerParams(vmem_limit_bytes=16 << 20),
    )(returned, weights)


def body(grads, momentum, weights):
    _, rows_dev, cols_dev = momentum.shape
    rows_total = rows_dev * lax.axis_size("fsdp")
    cols_total = cols_dev * lax.axis_size("dp")
    wide = cols_total // HALVES
    core = lax.axis_index("fsdp") % 2
    up1, down1 = pack(grads, momentum, wide, ((2, 0), (2, 1)), 59)
    up1, down1 = first_hop(up1, 1), first_hop(down1, -1)
    up2, down2 = pack(grads, momentum, wide, ((1, 1), (3, 0)), 59)
    up2, down2 = first_hop(up2, 1), first_hop(down2, -1)
    next_up, next_down, own0, own1 = pack(
        grads, momentum, wide, ((1, 0), (3, 1), (0, 0), (0, 1)), 48
    )
    up3, down3 = add_up(((next_up, up1), (next_down, down1)), False)
    up3, down3 = first_hop(up3, 1), first_hop(down3, -1)

    sums = add_up(((own0, down2, up3), (own1, up2, down3)), True)
    moments, groups = [], []
    for half in range(HALVES):
        parts = sums[SIDE * half : SIDE * (half + 1)]
        moment, sent = combine([parts[0]] + [second_hop(parts[k], k) for k in (1, 2, 3)])
        moments.append(moment)
        groups.append(gather(sent, core, half == 0))
    stop = rows_total * 9 // 11
    *before, zero = first_gram([groups[0][: RING - 1], groups[1][: RING - 1]], stop)
    last = groups[1][RING - 1]
    ends = [groups[0][RING - 1 :], [last, swap(last + zero)]]
    current = finish(ends, stop, moments, before)
    returned = lax.all_to_all(current, "dp", split_axis=0, concat_axis=0, tiled=True)
    return apply_update(returned, weights, 0.2 * math.sqrt(max(rows_total, cols_total)))


def solution(mesh):
    placed = (P("dp", None, "fsdp", None), P(None, "fsdp", "dp"), P(None, "fsdp", "dp"))
    return jax.shard_map(
        body,
        mesh=mesh,
        in_specs=placed,
        out_specs=(P(None, "fsdp", "dp"), P(None, "fsdp", "dp"), P(None, "fsdp", "dp")),
        check_vma=False,
    )
```

```python
import functools
import math

import jax
import jax.numpy as jnp
from jax import lax
from jax.experimental import pallas as pl
from jax.experimental.pallas import tpu as pltpu
from jax.sharding import PartitionSpec as P

SIDE = 4
RING = 8
PIECES = RING + 1
LANE = 128
HALVES = 2

MOMENTUM_DECAY = 0.95
LEARN_RATE = 0.02
DECAY_RATE = 0.1
COEF_A = 3.4445
COEF_B = -4.775
COEF_C = 2.0315
EPS_NORM = 1e-07
F32 = jnp.float32
BF16 = jnp.bfloat16
ROWS_BY_ROWS = (((1,), (1,)), ((), ()))
ANYWHERE = pl.BlockSpec(memory_space=pl.ANY)
IN_HBM = pl.BlockSpec(memory_space=pltpu.HBM)
IN_VMEM = pl.BlockSpec(memory_space=pltpu.VMEM)


def move(value, target):
    pairs = []
    for y in range(SIDE):
        for x in range(SIDE):
            for z in range(RING):
                for core in range(2):
                    ty, tx, tz, tc = target(y, x, z, core)
                    there = (((ty % SIDE) * SIDE + tx % SIDE) * RING + tz % RING) * 2 + tc % 2
                    pairs.append((((y * SIDE + x) * RING + z) * 2 + core, there))
    return lax.ppermute(value, ("dp", "fsdp"), pairs)


def first_hop(value, k):
    return move(value, lambda y, x, z, c: (y, x + k, z, c) if c == 0 else (y + k, x, z, c))


def second_hop(value, k):
    return move(value, lambda y, x, z, c: (y + k, x, z, c) if c == 0 else (y, x + k, z, c))


def along_z(value, k):
    return move(value, lambda y, x, z, c: (y, x, z + k, c) if c == 0 else (y, x, z - k, c))


def swap(value):
    return move(value, lambda y, x, z, c: (y, x, z, c + 1))


def cost(flops, size):
    return pl.CostEstimate(flops=flops, bytes_accessed=size, transcendentals=0)


def matrix(k, m):
    place = lax.axis_index("dp")
    y, x = place // SIDE, place % SIDE
    by_x = ((y + m) % SIDE) * SIDE + (x + k) % SIDE
    by_y = ((y + k) % SIDE) * SIDE + (x + m) % SIDE
    return jnp.where(lax.axis_index("fsdp") % 2 == 0, by_x, by_y)


def pack_kernel(wide, wanted, grads, mom, *refs):
    outs, terms, sems = refs[:-2], refs[-2], refs[-1]
    place = lax.axis_index("dp")
    per = wide // LANE
    cols = pl.ds(pl.multiple_of((place % per) * LANE, LANE), LANE)
    copies = []
    for i, (k, half) in enumerate(wanted):
        for m in range(SIDE):
            block = grads.at[0, matrix(k, m), :, pl.ds(half * wide, wide)]
            copies.append(pltpu.make_async_copy(block, outs[i].at[m], sems.at[0, i, m]))
            copies.append(pltpu.make_async_copy(mom.at[matrix(k, m)], terms.at[i, m], sems.at[1, i, m]))
    for copy in copies:
        copy.start()
    for copy in copies:
        copy.wait()
    for i, (_, half) in enumerate(wanted):

        @pl.when(place // per == half)
        def _():
            for m in range(SIDE):
                moment = MOMENTUM_DECAY * terms[i, m] + outs[i][m, :, cols].astype(F32)
                outs[i][m, :, cols] = moment.astype(BF16)


def pack(grads, momentum, wide, wanted, limit):
    rows = grads.shape[2]
    return pl.pallas_call(
        functools.partial(pack_kernel, wide, wanted),
        out_shape=(jax.ShapeDtypeStruct((SIDE, rows, wide), BF16),) * len(wanted),
        in_specs=[IN_HBM, IN_HBM],
        out_specs=(IN_VMEM,) * len(wanted),
        scratch_shapes=[
            pltpu.VMEM((len(wanted), SIDE, rows, LANE), F32),
            pltpu.SemaphoreType.DMA((2, len(wanted), SIDE)),
        ],
        compiler_params=pltpu.CompilerParams(vmem_limit_bytes=limit << 20),
        cost_estimate=cost(0, 4 * SIDE * rows * wide * len(wanted)),
    )(grads, momentum)


def add_kernel(count, split, *refs):
    inputs, outs = refs[: len(refs) - count[1]], refs[len(refs) - count[1] :]
    each = count[0]
    for place in range(len(inputs) // each):
        terms = inputs[place * each : (place + 1) * each]
        for m in range(SIDE):
            total = terms[0][m].astype(F32)
            for term in terms[1:]:
                total = total + term[m].astype(F32)
            if split:
                outs[place * SIDE + m][...] = total.astype(BF16)
            else:
                outs[place][m] = total.astype(BF16)


def add_up(groups, split):
    _, rows, wide = groups[0][0].shape
    if split:
        shape = (jax.ShapeDtypeStruct((rows, wide), BF16),) * (SIDE * len(groups))
    else:
        shape = (jax.ShapeDtypeStruct((SIDE, rows, wide), BF16),) * len(groups)
    inputs = [array for group in groups for array in group]
    return pl.pallas_call(
        functools.partial(add_kernel, (len(groups[0]), len(shape)), split),
        out_shape=shape,
        in_specs=[IN_VMEM] * len(inputs),
        out_specs=(IN_VMEM,) * len(shape),
        compiler_params=pltpu.CompilerParams(vmem_limit_bytes=16 << 20),
        cost_estimate=cost(0, 2 * SIDE * rows * wide * (len(inputs) + len(groups))),
    )(*inputs)


def combine_kernel(part0, part1, part2, part3, blocks, sent):
    for block in range(blocks.shape[0]):
        cols = slice(block * LANE, (block + 1) * LANE)
        total = part0[:, cols].astype(F32) + part1[:, cols].astype(F32)
        total = total + (part2[:, cols].astype(F32) + part3[:, cols].astype(F32))
        rounded = total.astype(BF16)
        blocks[block] = rounded
        sent[:, cols] = rounded


def combine(parts):
    rows, wide = parts[0].shape
    return pl.pallas_call(
        combine_kernel,
        out_shape=(
            jax.ShapeDtypeStruct((wide // LANE, rows, LANE), BF16),
            jax.ShapeDtypeStruct((rows, wide), BF16),
        ),
        in_specs=[IN_VMEM] * SIDE,
        out_specs=(IN_VMEM,) * 2,
        compiler_params=pltpu.CompilerParams(vmem_limit_bytes=16 << 20),
        cost_estimate=cost(0, 12 * rows * wide),
    )(*parts)


def gather(sent, core, whole):
    wide = sent.shape[1]
    same = along_z(sent, 1)
    cross = move(sent, lambda y, x, z, c: (y, x, z - 1, 1) if c == 0 else (y, x, z + 1, 0))
    other = swap(sent)
    chip, one = (
        jnp.concatenate([jnp.where(core == 0, mine, theirs), jnp.where(core == 0, theirs, mine)], axis=0)
        for mine, theirs in ((sent, other), (same, cross))
    )
    two = along_z(one, 1)
    three = along_z(two, 1)
    last = three
    if not whole:
        last = lax.dynamic_slice_in_dim(three, core * (wide // 2), wide // 2, axis=1)
    return [chip, one, swap(one), two, swap(two), three, swap(three), along_z(last, 1)]


def fetch(groups, begin, target, sems):
    core = lax.axis_index("fsdp") % 2
    copies = []
    for index, group in enumerate(groups):
        high, wide = target.shape[0] // RING, target.shape[1] // HALVES
        for place, piece in enumerate(group, begin):
            row, width, start = min(place, RING - 1) * high, piece.shape[1], index * wide
            if width < wide:
                right = core if place == RING - 1 else 1 - core
                start = pl.multiple_of(start + right * width, LANE)
            into = target.at[pl.ds(row, high), pl.ds(start, width)]
            copies.append(pltpu.make_async_copy(piece, into, sems.at[index, place]))
    for copy in copies:
        copy.start()
    return copies


def wait(copies):
    for copy in copies:
        copy.wait()


def gram_strip(rows, gram, at, end):
    term = lax.dot_general(
        rows[at:end, :], rows[0:end, :], ROWS_BY_ROWS, preferred_element_type=F32
    ).astype(BF16)
    gram[at:end, 0:end] = term
    if at:
        gram[0:at, at:end] = term[:, :at].T


def split(refs, counts):
    first, second = counts
    return (refs[:first], refs[first : first + second]), refs[first + second :]


def gram_kernel(counts, stop, *refs):
    groups, (rows, gram, zero, sems) = split(refs, counts)
    wait(fetch(groups, 0, rows, sems))
    for at in range(0, stop, 256):
        gram_strip(rows, gram, at, min(at + 256, stop))
    zero[...] = jnp.zeros(zero.shape, BF16)


def first_gram(groups, stop):
    high, wide = groups[0][0].shape
    size = RING * high
    pieces = [piece for group in groups for piece in group]
    return pl.pallas_call(
        functools.partial(gram_kernel, [len(group) for group in groups], stop),
        out_shape=(
            jax.ShapeDtypeStruct((size, HALVES * wide), BF16),
            jax.ShapeDtypeStruct((size, size), BF16),
            jax.ShapeDtypeStruct((high, wide // 2), BF16),
        ),
        in_specs=[ANYWHERE] * len(pieces),
        out_specs=(IN_VMEM,) * 3,
        scratch_shapes=[pltpu.SemaphoreType.DMA((HALVES, PIECES))],
        compiler_params=pltpu.CompilerParams(vmem_limit_bytes=24 << 20),
        cost_estimate=cost(stop * stop * wide * HALVES, 2 * len(pieces) * high * wide),
    )(*pieces)


def finish_kernel(counts, start, *refs):
    groups, refs = split(refs, counts)
    moments, (_, _, out, rows, gram, current, result, sems) = refs[:HALVES], refs[HALVES:]
    copies = fetch(groups, RING - 1, rows, sems)
    size, cols = rows.shape
    own = out.shape[2]
    for half, moment in enumerate(moments):
        for block in range(moment.shape[0]):
            out[half * moment.shape[0] + block, 0] = moment[block]
    wait(copies)
    for at in range(start, size, 256):
        gram_strip(rows, gram, at, min(at + 256, size))
    total = jnp.zeros((1, 1), F32)
    for at in range(0, size, LANE):
        term = gram[at : at + LANE, at : at + LANE].astype(F32)
        here = lax.broadcasted_iota(jnp.int32, term.shape, 0)
        there = lax.broadcasted_iota(jnp.int32, term.shape, 1)
        total = total + jnp.sum(jnp.where(here == there, term, 0.0), keepdims=True)
    inverse = 1.0 / (jnp.sqrt(total) + EPS_NORM)

    first = (lax.axis_index("fsdp") % 2) * own
    chip = gram[0 : 2 * own, :].astype(F32)
    gram_rows = jnp.where(first == 0, chip[:own], chip[own:]) * inverse * inverse

    def times_gram(rest):
        rest = (rest * inverse).astype(BF16)
        return jnp.dot(rest, gram[...], preferred_element_type=F32) * inverse

    current[...] = COEF_B * gram_rows + COEF_C * times_gram(gram_rows)
    result[...] = COEF_A * current[...]

    @pl.loop(0, 2)
    def _(step):
        scalar = jnp.where(step == 0, COEF_A, 0.0)
        once = times_gram(current[...]) + scalar * gram_rows
        current[...] = COEF_A * current[...] + COEF_B * once + COEF_C * times_gram(once)
        value = times_gram(current[...]) + COEF_A * scalar * gram_rows
        once = times_gram(value)
        value = COEF_A * value + COEF_B * once + COEF_C * times_gram(once)
        result[...] += jnp.where(step == 0, COEF_B, COEF_C) * value
        current[...] = value

    rest = result[...]
    scalar = COEF_A * COEF_A
    finite = total < jnp.inf
    high = jnp.where(finite, rest * inverse, 0.0).astype(BF16)
    scalar = jnp.where(finite, scalar * inverse, 0.0)
    chip_rows = rows[0 : 2 * own, :].astype(F32)
    own_rows = jnp.where(first == 0, chip_rows[:own], chip_rows[own:])
    for at in range(0, cols, 512):
        term = jnp.dot(high, rows[:, at : at + 512], preferred_element_type=F32)
        term = (term + scalar * own_rows[:, at : at + 512]).astype(BF16)
        for col in range(0, 512, LANE):
            out[(at + col) // LANE, 1] = term[:, col : col + LANE]


def finish(groups, start, moments, before):
    size, cols = before[0].shape
    own = moments[0].shape[1]
    pieces = [piece for group in groups for piece in group]
    inputs = len(pieces) + len(moments)
    return pl.pallas_call(
        functools.partial(finish_kernel, [len(group) for group in groups], start),
        out_shape=(
            jax.ShapeDtypeStruct((cols // LANE, 2, own, LANE), BF16),
            jax.ShapeDtypeStruct((size, cols), BF16),
            jax.ShapeDtypeStruct((size, size), BF16),
        ),
        in_specs=[ANYWHERE] * len(pieces) + [IN_VMEM] * (len(moments) + 2),
        out_specs=(IN_VMEM,) * 3,
        scratch_shapes=[
            pltpu.VMEM((own, size), F32),
            pltpu.VMEM((own, size), F32),
            pltpu.SemaphoreType.DMA((HALVES, PIECES)),
        ],
        input_output_aliases={inputs: 1, inputs + 1: 2},
        compiler_params=pltpu.CompilerParams(vmem_limit_bytes=32 << 20),
        cost_estimate=cost(26 * own * size * size + size * size * cols, 2 * size * (size + cols)),
    )(*pieces, *moments, *before)[0]


def update_kernel(scale, returned, weights, moment_new, new_weights, update):
    moment_new[...] = returned[:, 0].astype(F32)
    direction = scale * returned[:, 1].astype(F32)
    update[...] = direction.astype(BF16)
    kept = weights[...].astype(F32) * (1.0 - LEARN_RATE * DECAY_RATE)
    new_weights[...] = (kept - LEARN_RATE * direction).astype(BF16)


def apply_update(returned, weights, scale):
    shape = weights.shape
    return pl.pallas_call(
        functools.partial(update_kernel, scale),
        out_shape=(
            jax.ShapeDtypeStruct(shape, F32),
            jax.ShapeDtypeStruct(shape, BF16),
            jax.ShapeDtypeStruct(shape, BF16),
        ),
        in_specs=[IN_VMEM] * 2,
        out_specs=(IN_VMEM,) * 3,
        compiler_params=pltpu.CompilerParams(vmem_limit_bytes=16 << 20),
    )(returned, weights)


def body(grads, momentum, weights):
    _, rows_dev, cols_dev = momentum.shape
    rows_total = rows_dev * lax.axis_size("fsdp")
    cols_total = cols_dev * lax.axis_size("dp")
    wide = cols_total // HALVES
    core = lax.axis_index("fsdp") % 2
    up1, down1 = pack(grads, momentum, wide, ((2, 0), (2, 1)), 59)
    up1, down1 = first_hop(up1, 1), first_hop(down1, -1)
    up2, down2 = pack(grads, momentum, wide, ((1, 1), (3, 0)), 59)
    up2, down2 = first_hop(up2, 1), first_hop(down2, -1)
    next_up, next_down, own0, own1 = pack(
        grads, momentum, wide, ((1, 0), (3, 1), (0, 0), (0, 1)), 48
    )
    up3, down3 = add_up(((next_up, up1), (next_down, down1)), False)
    up3, down3 = first_hop(up3, 1), first_hop(down3, -1)

    sums = add_up(((own0, down2, up3), (own1, up2, down3)), True)
    moments, groups = [], []
    for half in range(HALVES):
        parts = sums[SIDE * half : SIDE * (half + 1)]
        moment, sent = combine([parts[0]] + [second_hop(parts[k], k) for k in (1, 2, 3)])
        moments.append(moment)
        groups.append(gather(sent, core, True))
    stop = rows_total * 9 // 11
    *before, _ = first_gram([groups[0], groups[1][: RING - 1]], stop)
    ends = [[], groups[1][RING - 1 :]]
    current = finish(ends, stop, moments, before)
    returned = lax.all_to_all(current, "dp", split_axis=0, concat_axis=0, tiled=True)
    return apply_update(returned, weights, 0.2 * math.sqrt(max(rows_total, cols_total)))


def solution(mesh):
    placed = (P("dp", None, "fsdp", None), P(None, "fsdp", "dp"), P(None, "fsdp", "dp"))
    return jax.shard_map(
        body,
        mesh=mesh,
        in_specs=placed,
        out_specs=(P(None, "fsdp", "dp"), P(None, "fsdp", "dp"), P(None, "fsdp", "dp")),
        check_vma=False,
    )
```
